32 devices in a mesh: groups: 2 (over y), replica: 4 (over z), tensor: 4 (over x, core).
Axes of the slice: x: 2, y: 2, z: 4, core: 2. Of those that a mesh axis runs over, the one named last changes fastest.
Arguments:
- normed_token_rows: bfloat16 [6144, 8192], P(('groups', 'replica'), 'tensor'), parts along dimension 0, may hold values from -6 to 6
- request_adapter_index: int32 [192, 1], P(('groups', 'replica')), parts along dimension 0, may hold values from 0 to 3; in each aligned block of 24 rows (0 to 23, 24 to 47, ...) at most 12 rows name the same one
- request_span_index: int32 [192], P(('groups', 'replica')), parts along dimension 0, may hold values from 0 to 255
- key_matrix: bfloat16 [8192, 1024], P('tensor'), may hold values from -0.0625 to 0.0625
- adapter_down_factors: bfloat16 [4, 8192, 64], P('replica', 'tensor'), may hold values from -0.0625 to 0.0625
- adapter_up_factors: bfloat16 [4, 64, 1024], P('replica', None, 'tensor'), may hold values from -0.75 to 0.75
Outputs:
- keys_out: bfloat16 [6144, 1024], P(('groups', 'replica'), 'tensor'), parts along dimension 0
The draws below stay inside these ranges and needn't reach their ends.
There are 2 independent parts, one for each index of `groups`. The reference program is written for one: setup_inputs(seed, part) draws one part's arguments, and reference() takes and returns one part's arrays. A program takes and returns all parts, laid end to end along the dimension named above; an argument that names none is the same for every part. Nothing has to cross between parts.
Inputs may be any that keep to these rules, and one draw needn't show every extreme that they name: `request_adapter_index`: among the 24 requests of one replica no adapter is named more than 12 times; in every draw some replica names some adapter exactly 12 times.
All inputs are finite; a program needn't handle non-finite values.
Results may differ from the reference program's by a relative error of at most 0.0055.
Values may be sent and summed in bfloat16 or wider, within the bound.
A program may use at most 128 MiB of HBM per device.

```python
import math
import jax
import jax.numpy as jnp
import numpy as np
from jax import lax

MODEL_WIDTH = 8192
HEAD = 128
ADAPTER_RANK = 64
REQ_ROWS = 32
REQS = 24
KEY_FEATURES = 1024
REQUESTS = 96
TOKENS = 3072
ADAPTER_COUNT = 4
CAP = 12


def place_ends(entries, key, least, largest):
    dims = entries.shape
    place = [jax.random.randint(jax.random.fold_in(key, axis), (), 0, dims[axis]) for axis in range(len(dims))]
    entries = entries.at[tuple(place)].set(least)
    longest = dims.index(max(dims))
    place[longest] = (place[longest] + 1) % dims[longest]
    return entries.at[tuple(place)].set(largest)


def levels(rng, dims, cuts, smallest, largest):
    factor_of, own = 1.0, jax.random.fold_in(rng, 6)
    for dim, shards_of in cuts:
        steps = jnp.exp(jax.random.uniform(jax.random.fold_in(own, dim), (shards_of,), jnp.float32, smallest / len(cuts), largest / len(cuts)))
        factor_of = factor_of * jnp.repeat(steps, dims[dim] // shards_of).reshape([-1 if axis == dim else 1 for axis in range(len(dims))])
    return factor_of


def assign_block(own_key, own, number, rows, count, top, reach, lean):
    sequence = jax.random.permutation(own_key, count)
    crowded, common = portions_of(count, rows * top, reach, lean, True), portions_of(count, rows * top, reach, lean, False)
    places = jnp.arange(count)

    def named(lengths, rotation):
        used = int((lengths > 0).sum())
        fixed = max(1, used // 4)
        passed = fixed + (places - fixed + rotation * (used - fixed)) % max(1, count - fixed)
        return jnp.zeros((count,), jnp.int32).at[sequence[jnp.where(places < fixed, places, passed)]].set(jnp.asarray(lengths, jnp.int32))

    lengths = jnp.where(number % 4 == 0, named(crowded, number // 4), named(common, number - number // 4 - 1))
    mixed = jax.random.permutation(jax.random.fold_in(own, 3), count)
    source_of, receiver = mixed[0:count // 2 * 2:2], mixed[1:count // 2 * 2:2]
    margin = jnp.minimum(lengths[source_of] - 1, reach - lengths[receiver]) // 2
    margin = jnp.where((source_of == sequence[0]) | (receiver == sequence[0]) | (lengths[receiver] == 0), 0, jnp.maximum(margin, 0))
    passed = jax.random.randint(jax.random.fold_in(own, 4), (count // 2,), 0, 1 << 20) % (margin + 1)
    lengths = lengths.at[source_of].add(-passed).at[receiver].add(passed)
    members = jnp.searchsorted(jnp.cumsum(lengths), jnp.arange(rows * top), side="right").astype(jnp.int32)
    table = members.reshape(top, rows).T
    table = table[jax.random.permutation(jax.random.fold_in(own, 1), rows)]
    rotation = jax.random.randint(jax.random.fold_in(own, 2), (rows, 1), 0, top)
    return jnp.take_along_axis(table, (jnp.arange(top)[None, :] + rotation) % top, axis=1)


def portions_of(number_of, total, reach, slope, full):
    portions = [(1 << 20) // math.isqrt(standing ** slope) + 1 for standing in range(1, number_of + 1)]
    largest = reach if full else min(reach, max(-(-total // number_of), total * portions[0] // sum(portions)))
    least = 1 if total - largest >= number_of - 1 else 0
    counts, surplus = [largest] + [least] * (number_of - 1), total - largest - least * (number_of - 1)
    while surplus > 0:
        free = [i for i in range(1, number_of) if counts[i] < largest] or [i for i in range(1, number_of) if counts[i] < reach]
        whole, remaining = sum([portions[i] for i in free]), surplus
        for i in free:
            extra = min(reach - counts[i], max(1, remaining * portions[i] // whole), surplus)
            counts[i] = counts[i] + extra
            surplus = surplus - extra
    return np.array(counts)


def normal_values(own_key, shape, deviation, bound, pieces=(), held_as=jnp.bfloat16):
    loudness = levels(own_key, shape, pieces, -0.22, 0.18) if pieces else 1.0
    array = jax.random.normal(own_key, shape, jnp.float32) * deviation * loudness
    return jnp.minimum(jnp.maximum(array, -bound), bound).astype(held_as)


def setup_inputs(seed: int = 0, part: int = 0) -> dict:
    key_list = jax.random.split(jax.random.key(seed), 7)
    part_splits = jax.random.split(jax.random.fold_in(key_list[6], part), 7)
    normed_token_rows = normal_values(part_splits[0], (TOKENS, MODEL_WIDTH), 1.0, 6.0, ((0, 4), (1, 4)))
    request_adapter_index_keys = jax.random.split(jax.random.fold_in(part_splits[1], 1), REQUESTS // REQS)
    request_adapter_index_turns = jax.random.permutation(jax.random.fold_in(part_splits[1], 3), REQUESTS // REQS)
    request_adapter_index = jax.vmap(lambda own, number: assign_block(jax.random.fold_in(part_splits[1], 2), own, number, REQS, ADAPTER_COUNT, 1, CAP, 2))(request_adapter_index_keys, request_adapter_index_turns).reshape((REQUESTS, 1))
    request_span_index = place_ends(jax.random.randint(part_splits[2], (REQUESTS,), 0, 8192 // REQ_ROWS), jax.random.fold_in(part_splits[2], 1), 0, (8192 // REQ_ROWS) - 1).astype(jnp.int32)
    key_matrix = normal_values(key_list[3], (MODEL_WIDTH, KEY_FEATURES), MODEL_WIDTH ** -0.5, 0.0625, ((0, 4),))
    adapter_down_factors = normal_values(key_list[4], (ADAPTER_COUNT, MODEL_WIDTH, ADAPTER_RANK), MODEL_WIDTH ** -0.5, 0.0625, ((0, 4), (1, 4)))
    adapter_up_factors = normal_values(key_list[5], (ADAPTER_COUNT, ADAPTER_RANK, KEY_FEATURES), ADAPTER_RANK ** -0.5, 0.75, ((0, 4), (2, 4)))
    return {"normed_token_rows": normed_token_rows, "request_adapter_index": request_adapter_index, "request_span_index": request_span_index, "key_matrix": key_matrix, "adapter_down_factors": adapter_down_factors, "adapter_up_factors": adapter_up_factors}


theta_base = 500000.0
adapter_scale = 2.0


def rotate(before, position):
    rows = before.shape[0]
    heads = before.reshape(rows, -1, HEAD)
    half = HEAD // 2
    freq = theta_base ** (-(jnp.arange(half).astype(jnp.float32) * 2.0 / HEAD))
    angle = position.astype(jnp.float32)[:, None] * freq[None, :]
    cosine = jnp.cos(angle)[:, None, :]
    sine = jnp.sin(angle)[:, None, :]
    first = heads[..., :half]
    second = heads[..., half:]
    turned = jnp.concatenate([first * cosine - second * sine, second * cosine + first * sine], axis=-1)
    return turned.reshape(rows, -1)


def reference(normed_token_rows, request_adapter_index, request_span_index, key_matrix, adapter_down_factors, adapter_up_factors):
    base = jnp.dot(normed_token_rows, key_matrix, preferred_element_type=jnp.float32)
    grouped = normed_token_rows.reshape(REQUESTS, REQ_ROWS, MODEL_WIDTH)

    def one_request(index):
        chosen_adapter = request_adapter_index[index, 0]
        rows_here = lax.dynamic_index_in_dim(grouped, index, 0, keepdims=False)
        down_factor = lax.dynamic_index_in_dim(adapter_down_factors, chosen_adapter, 0, keepdims=False)
        up_factor = lax.dynamic_index_in_dim(adapter_up_factors, chosen_adapter, 0, keepdims=False)
        reduced_rows = jnp.dot(rows_here, down_factor, preferred_element_type=jnp.float32).astype(jnp.bfloat16)
        return (jnp.dot(reduced_rows, up_factor, preferred_element_type=jnp.float32) * adapter_scale).astype(jnp.bfloat16)

    delta = lax.map(one_request, jnp.arange(REQUESTS, dtype=jnp.int32))
    before = base + delta.reshape(TOKENS, KEY_FEATURES).astype(jnp.float32)
    position = (request_span_index[:, None] * REQ_ROWS + jnp.arange(REQ_ROWS, dtype=jnp.int32)[None, :]).reshape(TOKENS)
    return rotate(before, position).astype(jnp.bfloat16)
```

```python
import functools
import math

import jax
import jax.numpy as jnp
from jax import lax
from jax.experimental import pallas as pl
from jax.experimental.pallas import tpu as pltpu
from jax.sharding import PartitionSpec as P

HEAD = 128
THETA = 500000.0
SCALE = 2.0
MESH = pl.DeviceIdType.MESH


def kernel(
    sizes,
    x_hbm, adapter_ref, span_ref, k_hbm, down_hbm, up_hbm,
    out_ref,
    xbuf, kbuf, downs, ups, mine, osend, orecv, xsend, xrecv,
    zacc, zsend, zrecv, zchip, zx, rowadapter, cosine, sine, angles,
    x_sem, k_sem, own_sem,
    down_ssem, down_rsem, fwd_ssem, fwd_rsem, up_ssem, up_rsem,
    o_ssem, o_rsem, xs_sem, xr_sem, z_ssem, z_rsem, zx_ssem, zx_rsem,
):
    groups, replicas, chips, chunks = sizes
    rows, width = xbuf.shape
    step = rows // chunks
    rank = downs.shape[1]
    part = rank // groups
    cols = ups.shape[2]
    requests = span_ref.shape[0]
    span_rows = rows // requests
    y = lax.axis_index("groups")
    z = lax.axis_index("replica")
    t = lax.axis_index("tensor")
    x, core = t // 2, t % 2
    partner = x * 2 + (1 - core)

    def chip_at(d):
        return lax.rem(x + d, chips)

    order = list(range(1, chips)) + [0]

    loads = {}
    for d in order:
        for j, who in ((0, 1 - core), (1, core)):
            start = pl.multiple_of((chip_at(d) * 2 + who) * cols, cols)
            loads["k", d, j] = pltpu.make_async_copy(
                k_hbm.at[:, pl.ds(start, cols)],
                kbuf.at[d, :, pl.ds(j * cols, cols)],
                k_sem.at[d, j],
            )
    for m in range(chunks):
        loads["x", m] = pltpu.make_async_copy(
            x_hbm.at[pl.ds(m * step, step)], xbuf.at[pl.ds(m * step, step)], x_sem.at[m]
        )
    loads["down"] = pltpu.make_async_copy(down_hbm, downs.at[z], own_sem.at[0])
    loads["up"] = pltpu.make_async_copy(up_hbm, ups.at[z], own_sem.at[1])
    first = order[0]
    loads["k", first, 0].start()
    loads["k", first, 1].start()
    for m in range(chunks):
        loads["x", m].start()
    for d in order[1:]:
        loads["k", d, 0].start()
        loads["k", d, 1].start()
    loads["down"].start()
    loads["up"].start()

    barrier = pltpu.get_barrier_semaphore()
    peers = 0
    for d in range(1, 2 * chips):
        pl.semaphore_signal(barrier, inc=1, device_id={"tensor": lax.rem(t + d, 2 * chips)}, device_id_type=MESH)
        peers += 1
    for d in range(1, replicas):
        pl.semaphore_signal(barrier, inc=1, device_id={"replica": lax.rem(z + d, replicas)}, device_id_type=MESH)
        peers += 1
    for d in range(1, groups):
        pl.semaphore_signal(barrier, inc=1, device_id={"groups": lax.rem(y + d, groups)}, device_id_type=MESH)
        peers += 1
    pl.semaphore_wait(barrier, peers)

    my_part = pl.ds(pl.multiple_of(y * part, part), part)
    for d in range(1, replicas):
        pltpu.make_async_remote_copy(
            src_ref=down_hbm.at[my_part], dst_ref=downs.at[z, my_part],
            send_sem=down_ssem.at[d], recv_sem=down_rsem.at[d],
            device_id={"replica": lax.rem(z + d, replicas)}, device_id_type=MESH,
        ).start()
    for d in range(1, replicas):
        pltpu.make_async_remote_copy(
            src_ref=up_hbm, dst_ref=ups.at[z],
            send_sem=up_ssem.at[d], recv_sem=up_rsem.at[d],
            device_id={"replica": lax.rem(z + d, replicas)}, device_id_type=MESH,
        ).start()

    def down_wait(d):
        return pltpu.make_async_remote_copy(
            src_ref=down_hbm.at[my_part],
            dst_ref=downs.at[lax.rem(z - d + replicas, replicas), my_part],
            send_sem=down_ssem.at[d], recv_sem=down_rsem.at[d],
            device_id={"replica": lax.rem(z + d, replicas)}, device_id_type=MESH,
        )

    def up_wait(d):
        return pltpu.make_async_remote_copy(
            src_ref=up_hbm, dst_ref=ups.at[lax.rem(z - d + replicas, replicas)],
            send_sem=up_ssem.at[d], recv_sem=up_rsem.at[d],
            device_id={"replica": lax.rem(z + d, replicas)}, device_id_type=MESH,
        )

    def forward(d, g):
        source = lax.rem(z - d + replicas, replicas)
        return pltpu.make_async_remote_copy(
            src_ref=downs.at[source, my_part], dst_ref=downs.at[source, my_part],
            send_sem=fwd_ssem.at[d, g], recv_sem=fwd_rsem.at[d, g],
            device_id={"groups": lax.rem(y + g, groups)}, device_id_type=MESH,
        )

    def forward_wait(d, g):
        source = lax.rem(z - d + replicas, replicas)
        theirs = pl.ds(pl.multiple_of(lax.rem(y - g + groups, groups) * part, part), part)
        return pltpu.make_async_remote_copy(
            src_ref=downs.at[source, theirs], dst_ref=downs.at[source, theirs],
            send_sem=fwd_ssem.at[d, g], recv_sem=fwd_rsem.at[d, g],
            device_id={"groups": lax.rem(y + g, groups)}, device_id_type=MESH,
        )

    def to_partner(d, m):
        rs = pl.ds(m * step, step)
        return pltpu.make_async_remote_copy(
            src_ref=osend.at[d, rs], dst_ref=orecv.at[d, rs],
            send_sem=o_ssem.at[d, m], recv_sem=o_rsem.at[d, m],
            device_id={"tensor": partner}, device_id_type=MESH,
        )

    def to_chip(d, m):
        rs = pl.ds(m * step, step)
        return pltpu.make_async_remote_copy(
            src_ref=xsend.at[d, rs], dst_ref=xrecv.at[d, rs],
            send_sem=xs_sem.at[d, m], recv_sem=xr_sem.at[d, m],
            device_id={"tensor": chip_at(d) * 2 + core}, device_id_type=MESH,
        )

    def product(d, m):
        if (d, m) == (order[0], 0):
            loads["k", d, 0].wait()
            loads["k", d, 1].wait()
        elif m == 0:
            loads["k", d, 0].wait()
            loads["k", d, 1].wait()
        if d == order[0]:
            loads["x", m].wait()
        rs = pl.ds(m * step, step)
        both = jnp.dot(xbuf[rs, :], kbuf[d], preferred_element_type=jnp.float32)
        osend[d, rs, :] = both[:, :cols].astype(jnp.bfloat16)
        to_partner(d, m).start()
        mine[d, rs, :] = both[:, cols:]

    def pass_on(d, m):
        rs = pl.ds(m * step, step)
        to_partner(d, m).wait()
        if d != 0:
            total = mine[d, rs, :] + orecv[d, rs, :].astype(jnp.float32)
            xsend[d, rs, :] = total.astype(jnp.bfloat16)
            to_chip(d, m).start()

    todo = [(d, m) for d in order for m in range(chunks)]
    for i, (d, m) in enumerate(todo):
        product(d, m)
        if i >= 1:
            pass_on(*todo[i - 1])

    for q in range(requests):
        rowadapter[pl.ds(q * span_rows, span_rows), :] = jnp.full((span_rows, rank), adapter_ref[q], jnp.int32)
        angles[pl.ds(q, 1), :] = jnp.full((1, HEAD), span_ref[q] * span_rows, jnp.int32).astype(jnp.float32)
    lane = lax.broadcasted_iota(jnp.int32, (1, HEAD), 1)
    half = HEAD // 2
    index = jnp.where(lane >= half, lane - half, lane).astype(jnp.float32)
    freq = jnp.exp(index * (-2.0 / HEAD * math.log(THETA)))
    sign = jnp.where(lane >= half, 1.0, -1.0)
    start_angle = angles[...] * freq
    row_angle = lax.broadcasted_iota(jnp.int32, (span_rows, HEAD), 0).astype(jnp.float32) * freq
    cos_a, sin_a = jnp.cos(start_angle), jnp.sin(start_angle)
    cos_b, sin_b = jnp.cos(row_angle), jnp.sin(row_angle)
    for q in range(requests):
        rs = pl.ds(q * span_rows, span_rows)
        ca, sa = cos_a[q : q + 1, :], sin_a[q : q + 1, :]
        cosine[rs, :] = ca * cos_b - sa * sin_b
        sine[rs, :] = sign * (sa * cos_b + ca * sin_b)

    def shrink(a, initial):
        value = lax.dot_general(
            xbuf[...], downs[a], (((1,), (1,)), ((), ())), preferred_element_type=jnp.float32
        )
        chosen = jnp.where(rowadapter[...] == a, value, 0.0)
        if initial:
            zacc[...] = chosen
        else:
            zacc[...] += chosen

    loads["down"].wait()
    shrink(z, True)
    pass_on(*todo[-1])
    for d in range(1, replicas):
        down_wait(d).wait()
        for g in range(1, groups):
            forward(d, g).start()
    for d in range(1, replicas):
        for g in range(1, groups):
            forward_wait(d, g).wait()
        shrink(lax.rem(z - d + replicas, replicas), False)

    mid = rows // 2
    quarter = rows // 4
    packed = jnp.concatenate([zacc[:mid, :], zacc[mid:, :]], axis=1)
    for h in range(2):
        zsend[h] = packed[h * quarter : (h + 1) * quarter].astype(jnp.bfloat16)
    z_copy = pltpu.make_async_remote_copy(
        src_ref=zsend, dst_ref=zrecv, send_sem=z_ssem, recv_sem=z_rsem,
        device_id={"tensor": partner}, device_id_type=MESH,
    )
    z_copy.start()
    z_copy.wait()
    chip_sum = [
        packed[h * quarter : (h + 1) * quarter] + zrecv[h].astype(jnp.float32) for h in range(2)
    ]
    for h in range(2):
        zchip[h] = chip_sum[h].astype(jnp.bfloat16)

    def z_over(d, c):
        return pltpu.make_async_remote_copy(
            src_ref=zchip.at[core], dst_ref=zx.at[d, core],
            send_sem=zx_ssem.at[d, c], recv_sem=zx_rsem.at[d, core],
            device_id={"tensor": chip_at(d) * 2 + c}, device_id_type=MESH,
        )

    def z_arrival(d, c):
        return pltpu.make_async_remote_copy(
            src_ref=zchip.at[c], dst_ref=zx.at[d, c],
            send_sem=zx_ssem.at[d, c], recv_sem=zx_rsem.at[d, c],
            device_id={"tensor": chip_at(d) * 2 + c}, device_id_type=MESH,
        )

    for d in range(1, chips):
        for c in range(2):
            z_over(d, c).start()
    loads["up"].wait()
    for d in range(1, replicas):
        up_wait(d).wait()
    for d in range(1, chips):
        for c in range(2):
            z_arrival(d, c).wait()
    sums = []
    for h in range(2):
        total = chip_sum[h]
        for d in range(1, chips):
            total = total + zx[d, h].astype(jnp.float32)
        sums.append(total)
    packed = jnp.concatenate(sums, axis=0)
    shrunk = jnp.concatenate([packed[:, :rank], packed[:, rank:]], axis=0)

    together = 4 if replicas % 4 == 0 else 1
    for d in range(1, chips):
        for m in range(chunks):
            to_chip(d, m).wait()
    for m in range(chunks):
        rs = pl.ds(m * step, step)
        reduced = shrunk[m * step : (m + 1) * step]
        names = rowadapter[rs, :]
        expanded = jnp.zeros((step, cols), jnp.float32)
        for a in range(0, replicas, together):
            masked = [jnp.where(names == a + i, reduced, 0.0) for i in range(together)]
            masked = jnp.concatenate(masked, axis=1) if together > 1 else masked[0]
            expanded += jnp.dot(
                masked.astype(jnp.bfloat16),
                ups[a : a + together].reshape(together * rank, cols),
                preferred_element_type=jnp.float32,
            )
        delta = (expanded * SCALE).astype(jnp.bfloat16).astype(jnp.float32)
        base = mine[0, rs, :] + orecv[0, rs, :].astype(jnp.float32)
        for d in range(1, chips):
            base += xrecv[d, rs, :].astype(jnp.float32)
        before = base + delta
        for h in range(cols // HEAD):
            head = before[:, h * HEAD : (h + 1) * HEAD]
            turned = head * cosine[rs, :] + pltpu.roll(head, half, 1) * sine[rs, :]
            out_ref[rs, h * HEAD : (h + 1) * HEAD] = turned.astype(jnp.bfloat16)


def on_device(sizes, rows, adapters, spans, keys, down, up):
    groups, replicas, chips, chunks = sizes
    row_count, width = rows.shape
    rank, cols = up.shape[1], up.shape[2]
    requests = spans.shape[0]
    bf, f32 = jnp.bfloat16, jnp.float32
    vm, dma = pltpu.VMEM, pltpu.SemaphoreType.DMA
    quarter = row_count // 4
    anywhere = pl.BlockSpec(memory_space=pl.ANY)
    smem = pl.BlockSpec(memory_space=pltpu.SMEM)
    return pl.pallas_call(
        functools.partial(kernel, sizes),
        out_shape=jax.ShapeDtypeStruct((row_count, cols), bf),
        in_specs=[anywhere, smem, smem, anywhere, anywhere, anywhere],
        out_specs=pl.BlockSpec(memory_space=pltpu.VMEM),
        scratch_shapes=[
            vm((row_count, width), bf),
            vm((chips, width, 2 * cols), bf),
            vm((replicas, rank, width), bf),
            vm((replicas, rank, cols), bf),
            vm((chips, row_count, cols), f32),
            vm((chips, row_count, cols), bf),
            vm((chips, row_count, cols), bf),
            vm((chips, row_count, cols), bf),
            vm((chips, row_count, cols), bf),
            vm((row_count, rank), f32),
            vm((2, quarter, 2 * rank), bf),
            vm((2, quarter, 2 * rank), bf),
            vm((2, quarter, 2 * rank), bf),
            vm((chips, 2, quarter, 2 * rank), bf),
            vm((row_count, rank), jnp.int32),
            vm((row_count, HEAD), f32),
            vm((row_count, HEAD), f32),
            vm((requests, HEAD), f32),
            dma((chunks,)), dma((chips, 2)), dma((2,)),
            dma((replicas,)), dma((replicas,)),
            dma((replicas, groups)), dma((replicas, groups)),
            dma((replicas,)), dma((replicas,)),
            dma((chips, chunks)), dma((chips, chunks)),
            dma((chips, chunks)), dma((chips, chunks)),
            dma, dma,
            dma((chips, 2)), dma((chips, 2)),
        ],
        compiler_params=pltpu.CompilerParams(
            collective_id=0, has_side_effects=True, vmem_limit_bytes=48 * 1024 * 1024
        ),
        cost_estimate=pl.CostEstimate(
            flops=2 * row_count * width * (2 * chips * cols + replicas * rank),
            bytes_accessed=2 * width * (row_count + 2 * chips * cols),
            transcendentals=0,
        ),
    )(rows, adapters.reshape(requests), spans, keys, down[0].T, up[0])


def solution(mesh):
    in_specs = (
        P(("groups", "replica"), "tensor"),
        P(("groups", "replica"), None),
        P(("groups", "replica")),
        P("tensor", None),
        P("replica", "tensor", None),
        P("replica", None, "tensor"),
    )
    out_specs = P(("groups", "replica"), "tensor")
    sizes = (mesh.shape["groups"], mesh.shape["replica"], mesh.shape["tensor"] // 2, 3)
    return jax.shard_map(
        functools.partial(on_device, sizes), mesh=mesh, in_specs=in_specs, out_specs=out_specs, check_vma=False
    )
```

```python
import functools
import math

import jax
import jax.numpy as jnp
from jax import lax
from jax.experimental import pallas as pl
from jax.experimental.pallas import tpu as pltpu
from jax.sharding import PartitionSpec as P

HEAD = 128
THETA = 500000.0
SCALE = 2.0
TOGETHER = 4
MESH = pl.DeviceIdType.MESH


def kernel(
    sizes,
    x_hbm, adapter_ref, span_ref, k_hbm, down_hbm, up_hbm,
    out_ref,
    xbuf, kbuf, downs, ups, mine, osend, orecv, xsend, xrecv,
    zacc, zsend, zrecv, zchip, zx, rowadapter, cosine, sine, angles,
    x_sem, k_sem, own_sem,
    down_ssem, down_rsem, fwd_ssem, fwd_rsem, up_ssem, up_rsem,
    o_ssem, o_rsem, xs_sem, xr_sem, z_ssem, z_rsem, zx_ssem, zx_rsem,
):
    groups, replicas, chips, chunks, pieces = sizes
    rows, width = xbuf.shape
    step = rows // chunks
    rank = downs.shape[1]
    part = width // groups
    cols = ups.shape[2]
    requests = span_ref.shape[0]
    span_rows = rows // requests
    y = lax.axis_index("groups")
    z = lax.axis_index("replica")
    t = lax.axis_index("tensor")
    x, core = t // 2, t % 2
    partner = x * 2 + (1 - core)

    def chip_at(d):
        return lax.rem(x + d, chips)

    barrier = pltpu.get_barrier_semaphore()
    peers = 0
    for d in range(1, 2 * chips):
        pl.semaphore_signal(barrier, inc=1, device_id={"tensor": lax.rem(t + d, 2 * chips)}, device_id_type=MESH)
        peers += 1
    for d in range(1, replicas):
        pl.semaphore_signal(barrier, inc=1, device_id={"replica": lax.rem(z + d, replicas)}, device_id_type=MESH)
        peers += 1
    for d in range(1, groups):
        pl.semaphore_signal(barrier, inc=1, device_id={"groups": lax.rem(y + d, groups)}, device_id_type=MESH)
        peers += 1

    order = list(range(1, chips)) + [0]

    loads = {}
    for d in order:
        for j, who in ((0, 1 - core), (1, core)):
            start = pl.multiple_of((chip_at(d) * 2 + who) * cols, cols)
            loads["k", d, j] = pltpu.make_async_copy(
                k_hbm.at[:, pl.ds(start, cols)],
                kbuf.at[d, :, pl.ds(j * cols, cols)],
                k_sem.at[d, j],
            )
    for m in range(chunks):
        loads["x", m] = pltpu.make_async_copy(
            x_hbm.at[pl.ds(m * step, step)], xbuf.at[pl.ds(m * step, step)], x_sem.at[m]
        )
    loads["down"] = pltpu.make_async_copy(down_hbm, downs.at[z], own_sem.at[0])
    loads["up"] = pltpu.make_async_copy(up_hbm, ups.at[z], own_sem.at[1])
    first = order[0]
    loads["k", first, 0].start()
    loads["k", first, 1].start()
    for m in range(chunks):
        loads["x", m].start()
    for d in order[1:]:
        loads["k", d, 0].start()
        loads["k", d, 1].start()
    loads["down"].start()
    loads["up"].start()

    block_of = lax.broadcasted_iota(jnp.int32, (span_rows, TOGETHER * rank), 1) // rank
    for q in range(requests):
        rowadapter[pl.ds(q * span_rows, span_rows), :] = jnp.full((span_rows, TOGETHER * rank), adapter_ref[q], jnp.int32) - block_of
        angles[pl.ds(q, 1), :] = jnp.full((1, HEAD), span_ref[q] * span_rows, jnp.int32).astype(jnp.float32)
    lane = lax.broadcasted_iota(jnp.int32, (1, HEAD), 1)
    half = HEAD // 2
    index = jnp.where(lane >= half, lane - half, lane).astype(jnp.float32)
    freq = jnp.exp(index * (-2.0 / HEAD * math.log(THETA)))
    sign = jnp.where(lane >= half, 1.0, -1.0)
    start_angle = angles[...] * freq
    row_angle = lax.broadcasted_iota(jnp.int32, (span_rows, HEAD), 0).astype(jnp.float32) * freq
    cos_a, sin_a = jnp.cos(start_angle), jnp.sin(start_angle)
    cos_b, sin_b = jnp.cos(row_angle), jnp.sin(row_angle)
    for q in range(requests):
        rs = pl.ds(q * span_rows, span_rows)
        ca, sa = cos_a[q : q + 1, :], sin_a[q : q + 1, :]
        cosine[rs, :] = ca * cos_b - sa * sin_b
        sine[rs, :] = sign * (sa * cos_b + ca * sin_b)

    def product(d, m):
        if (d, m) == (order[0], 0):
            loads["k", d, 0].wait()
            loads["k", d, 1].wait()
        elif m == 0:
            loads["k", d, 0].wait()
            loads["k", d, 1].wait()
        if d == order[0]:
            loads["x", m].wait()
        rs = pl.ds(m * step, step)
        both = jnp.dot(xbuf[rs, :], kbuf[d], preferred_element_type=jnp.float32)
        osend[d, rs, :] = both[:, :cols].astype(jnp.bfloat16)
        mine[d, rs, :] = both[:, cols:]

    todo = [(d, m) for d in order for m in range(chunks)]
    pl.semaphore_wait(barrier, peers)

    def piece(g, p):
        at = lax.rem(y + g + groups, groups) * part + p * (part // pieces)
        return pl.ds(pl.multiple_of(at, 128), part // pieces)

    def group_part(g):
        return pl.ds(pl.multiple_of(lax.rem(y + g + groups, groups) * part, 128), part)

    def hop(a, p, way):
        return pltpu.make_async_remote_copy(
            src_ref=downs.at[a, :, piece(0, p)], dst_ref=downs.at[a, :, piece(0, p)],
            send_sem=down_ssem.at[a, p, (way + 1) // 2], recv_sem=down_rsem.at[a, p],
            device_id={"replica": z + way}, device_id_type=MESH,
        )

    def own_hop(p, way):
        return pltpu.make_async_remote_copy(
            src_ref=down_hbm.at[:, piece(0, p)], dst_ref=downs.at[z, :, piece(0, p)],
            send_sem=down_ssem.at[z, p, (way + 1) // 2], recv_sem=down_rsem.at[z, p],
            device_id={"replica": z + way}, device_id_type=MESH,
        )

    def forward(a, g, p, own):
        cut = piece(0 if own else -g, p)
        return pltpu.make_async_remote_copy(
            src_ref=downs.at[a, :, cut], dst_ref=downs.at[a, :, cut],
            send_sem=fwd_ssem.at[a, g, p], recv_sem=fwd_rsem.at[a, g, p],
            device_id={"groups": lax.rem(y + g, groups)}, device_id_type=MESH,
        )

    def relay(a, p, way):
        hop(a, p, way).wait_recv()
        pl.when((z + way >= 0) & (z + way < replicas))(lambda: hop(a, p, way).start())
        for g in range(1, groups):
            forward(a, g, p, True).start()

    def relay_from(k):
        for p in range(pieces):
            pl.when(z >= k)(lambda: relay(z - k, p, 1))
            pl.when(z + k < replicas)(lambda: relay(z + k, p, -1))

    def relay_end(k):
        for p in range(pieces):
            @pl.when((z >= k) & (z + 1 < replicas))
            def _():
                (own_hop(p, 1) if k == 0 else hop(z - k, p, 1)).wait_send()

            @pl.when((z + k < replicas) & (z >= 1))
            def _():
                (own_hop(p, -1) if k == 0 else hop(z + k, p, -1)).wait_send()

    def up_send(j):
        return pltpu.make_async_remote_copy(
            src_ref=up_hbm, dst_ref=ups.at[z],
            send_sem=up_ssem.at[j], recv_sem=up_rsem.at[j],
            device_id={"replica": lax.rem(z + j, replicas)}, device_id_type=MESH,
        )

    def up_arrival(j):
        return pltpu.make_async_remote_copy(
            src_ref=up_hbm, dst_ref=ups.at[lax.rem(z - j + replicas, replicas)],
            send_sem=up_ssem.at[j], recv_sem=up_rsem.at[j],
            device_id={"replica": lax.rem(z + j, replicas)}, device_id_type=MESH,
        )

    for p in range(pieces):
        pl.when(z + 1 < replicas)(lambda: own_hop(p, 1).start())
        pl.when(z >= 1)(lambda: own_hop(p, -1).start())

    def to_partner(d, m):
        rs = pl.ds(m * step, step)
        return pltpu.make_async_remote_copy(
            src_ref=osend.at[d, rs], dst_ref=orecv.at[d, rs],
            send_sem=o_ssem.at[d, m], recv_sem=o_rsem.at[d, m],
            device_id={"tensor": partner}, device_id_type=MESH,
        )

    def to_chip(d, m):
        rs = pl.ds(m * step, step)
        return pltpu.make_async_remote_copy(
            src_ref=xsend.at[d, rs], dst_ref=xrecv.at[d, rs],
            send_sem=xs_sem.at[d, m], recv_sem=xr_sem.at[d, m],
            device_id={"tensor": chip_at(d) * 2 + core}, device_id_type=MESH,
        )

    def pass_on(d, m):
        rs = pl.ds(m * step, step)
        to_partner(d, m).wait()
        if d != 0:
            total = mine[d, rs, :] + orecv[d, rs, :].astype(jnp.float32)
            xsend[d, rs, :] = total.astype(jnp.bfloat16)
            to_chip(d, m).start()

    hops = 1
    for i, (d, m) in enumerate(todo):
        product(d, m)
        to_partner(d, m).start()
        if i >= 1:
            pass_on(*todo[i - 1])
        if i + 1 >= chunks and hops < replicas:
            relay_from(hops)
            hops += 1
    for k in range(hops, replicas):
        relay_from(k)
    for j in range(1, replicas):
        up_send(j).start()
    pass_on(*todo[-1])

    def shrink(cut):
        kept = None
        for a in range(0, replicas, TOGETHER):
            value = lax.dot_general(
                xbuf[:, cut],
                downs[a : a + TOGETHER, :, cut].reshape(TOGETHER * rank, part),
                (((1,), (1,)), ((), ())),
                preferred_element_type=jnp.float32,
            )
            chosen = jnp.where(rowadapter[...] == a, value, 0.0)
            kept = chosen if kept is None else kept + chosen
        pair = kept[:, : 2 * rank] + kept[:, 2 * rank :]
        return pair + pltpu.roll(pair, rank, 1)

    loads["down"].wait()
    zacc[...] = shrink(group_part(0))
    for m in range(chunks):
        rs = pl.ds(m * step, step)
        base = mine[0, rs, :] + orecv[0, rs, :].astype(jnp.float32)
        for d in range(1, chips):
            to_chip(d, m).wait()
            base += xrecv[d, rs, :].astype(jnp.float32)
        mine[0, rs, :] = base
    for g in range(1, groups):
        for j in range(1, replicas):
            for p in range(pieces):
                forward(lax.rem(z + j, replicas), g, p, False).wait_recv()
    for g in range(1, groups):
        zacc[...] += shrink(group_part(-g))

    mid = rows // 2
    quarter = rows // 4
    low = lax.broadcasted_iota(jnp.int32, (mid, 2 * rank), 1) < rank
    packed = jnp.where(low, zacc[:mid, :], zacc[mid:, :])
    for h in range(2):
        zsend[h] = packed[h * quarter : (h + 1) * quarter].astype(jnp.bfloat16)
    z_copy = pltpu.make_async_remote_copy(
        src_ref=zsend, dst_ref=zrecv, send_sem=z_ssem, recv_sem=z_rsem,
        device_id={"tensor": partner}, device_id_type=MESH,
    )
    z_copy.start()
    z_copy.wait()
    chip_sum = [
        packed[h * quarter : (h + 1) * quarter] + zrecv[h].astype(jnp.float32) for h in range(2)
    ]
    for h in range(2):
        zchip[h] = chip_sum[h].astype(jnp.bfloat16)

    def z_over(d, c):
        return pltpu.make_async_remote_copy(
            src_ref=zchip.at[core], dst_ref=zx.at[d, core],
            send_sem=zx_ssem.at[d, c], recv_sem=zx_rsem.at[d, core],
            device_id={"tensor": chip_at(d) * 2 + c}, device_id_type=MESH,
        )

    def z_arrival(d, c):
        return pltpu.make_async_remote_copy(
            src_ref=zchip.at[c], dst_ref=zx.at[d, c],
            send_sem=zx_ssem.at[d, c], recv_sem=zx_rsem.at[d, c],
            device_id={"tensor": chip_at(d) * 2 + c}, device_id_type=MESH,
        )

    for d in range(1, chips):
        for c in range(2):
            z_over(d, c).start()
    loads["up"].wait()
    for j in range(1, replicas):
        up_arrival(j).wait()
    for k in range(replicas):
        relay_end(k)
    for g in range(1, groups):
        for j in range(1, replicas):
            for p in range(pieces):
                forward(lax.rem(z + j, replicas), g, p, True).wait_send()
    for d in range(1, chips):
        for c in range(2):
            z_arrival(d, c).wait()
    sums = []
    for h in range(2):
        total = chip_sum[h]
        for d in range(1, chips):
            total = total + zx[d, h].astype(jnp.float32)
        sums.append(total)
    packed = jnp.concatenate(sums, axis=0)
    swapped = pltpu.roll(packed, rank, 1)
    shrunk = jnp.concatenate([jnp.where(low, packed, swapped), jnp.where(low, swapped, packed)], axis=0)
    shrunk = jnp.concatenate([shrunk] * (TOGETHER // 2), axis=1)

    for m in range(chunks):
        rs = pl.ds(m * step, step)
        reduced = shrunk[m * step : (m + 1) * step]
        names = rowadapter[rs, :]
        expanded = jnp.zeros((step, cols), jnp.float32)
        for a in range(0, replicas, TOGETHER):
            expanded += jnp.dot(
                jnp.where(names == a, reduced, 0.0).astype(jnp.bfloat16),
                ups[a : a + TOGETHER].reshape(TOGETHER * rank, cols),
                preferred_element_type=jnp.float32,
            )
        delta = (expanded * SCALE).astype(jnp.bfloat16).astype(jnp.float32)
        before = mine[0, rs, :] + delta
        for h in range(cols // HEAD):
            head = before[:, h * HEAD : (h + 1) * HEAD]
            turned = head * cosine[rs, :] + pltpu.roll(head, half, 1) * sine[rs, :]
            out_ref[rs, h * HEAD : (h + 1) * HEAD] = turned.astype(jnp.bfloat16)


def on_device(sizes, rows, adapters, spans, keys, down, up):
    groups, replicas, chips, chunks, pieces = sizes
    row_count, width = rows.shape
    rank, cols = up.shape[1], up.shape[2]
    requests = spans.shape[0]
    bf, f32 = jnp.bfloat16, jnp.float32
    vm, dma = pltpu.VMEM, pltpu.SemaphoreType.DMA
    quarter = row_count // 4
    anywhere = pl.BlockSpec(memory_space=pltpu.HBM)
    smem = pl.BlockSpec(memory_space=pltpu.SMEM)
    return pl.pallas_call(
        functools.partial(kernel, sizes),
        out_shape=jax.ShapeDtypeStruct((row_count, cols), bf),
        in_specs=[anywhere, smem, smem, anywhere, anywhere, anywhere],
        out_specs=pl.BlockSpec(memory_space=pltpu.VMEM),
        scratch_shapes=[
            vm((row_count, width), bf),
            vm((chips, width, 2 * cols), bf),
            vm((replicas, rank, width), bf),
            vm((replicas, rank, cols), bf),
            vm((chips, row_count, cols), f32),
            vm((chips, row_count, cols), bf),
            vm((chips, row_count, cols), bf),
            vm((chips, row_count, cols), bf),
            vm((chips, row_count, cols), bf),
            vm((row_count, 2 * rank), f32),
            vm((2, quarter, 2 * rank), bf),
            vm((2, quarter, 2 * rank), bf),
            vm((2, quarter, 2 * rank), bf),
            vm((chips, 2, quarter, 2 * rank), bf),
            vm((row_count, TOGETHER * rank), jnp.int32),
            vm((row_count, HEAD), f32),
            vm((row_count, HEAD), f32),
            vm((requests, HEAD), f32),
            dma((chunks,)), dma((chips, 2)), dma((2,)),
            dma((replicas, pieces, 2)), dma((replicas, pieces)),
            dma((replicas, groups, pieces)), dma((replicas, groups, pieces)),
            dma((replicas,)), dma((replicas,)),
            dma((chips, chunks)), dma((chips, chunks)),
            dma((chips, chunks)), dma((chips, chunks)),
            dma, dma,
            dma((chips, 2)), dma((chips, 2)),
        ],
        compiler_params=pltpu.CompilerParams(
            collective_id=0, has_side_effects=True, vmem_limit_bytes=60 * 1024 * 1024
        ),
        cost_estimate=pl.CostEstimate(
            flops=2 * row_count * width * (2 * chips * cols + replicas * rank),
            bytes_accessed=2 * width * (row_count + 2 * chips * cols),
            transcendentals=0,
        ),
    )(rows, adapters.reshape(requests), spans, keys, down[0].T, up[0])


def solution(mesh):
    in_specs = (
        P(("groups", "replica"), "tensor"),
        P(("groups", "replica"), None),
        P(("groups", "replica")),
        P("tensor", None),
        P("replica", "tensor", None),
        P("replica", None, "tensor"),
    )
    out_specs = P(("groups", "replica"), "tensor")
    sizes = (mesh.shape["groups"], mesh.shape["replica"], mesh.shape["tensor"] // 2, 3)
    sizes += (max(1, 16 // sizes[1]),)
    return jax.shard_map(
        functools.partial(on_device, sizes), mesh=mesh, in_specs=in_specs, out_specs=out_specs, check_vma=False
    )
```

```python
import functools
import math

import jax
import jax.numpy as jnp
from jax import lax
from jax.experimental import pallas as pl
from jax.experimental.pallas import tpu as pltpu
from jax.sharding import PartitionSpec as P

HEAD = 128
THETA = 500000.0
SCALE = 2.0
TOGETHER = 4
MESH = pl.DeviceIdType.MESH


def kernel(
    sizes,
    x_hbm, adapter_ref, span_ref, k_hbm, down_hbm, up_hbm,
    out_ref,
    xbuf, kbuf, downs, ups, mine, osend, orecv, xsend, xrecv,
    zacc, zsend, zrecv, zchip, zx, rowadapter, cosine, sine, angles,
    x_sem, k_sem, own_sem,
    down_ssem, down_rsem, fwd_ssem, fwd_rsem, up_ssem, up_rsem,
    o_ssem, o_rsem, xs_sem, xr_sem, z_ssem, z_rsem, zx_ssem, zx_rsem,
):
    groups, replicas, chips, chunks, pieces = sizes
    rows, width = xbuf.shape
    step = rows // chunks
    rank = downs.shape[1]
    part = width // groups
    cols = ups.shape[2]
    requests = span_ref.shape[0]
    span_rows = rows // requests
    y = lax.axis_index("groups")
    z = lax.axis_index("replica")
    t = lax.axis_index("tensor")
    x, core = t // 2, t % 2
    partner = x * 2 + (1 - core)

    def chip_at(d):
        return lax.rem(x + d, chips)

    barrier = pltpu.get_barrier_semaphore()
    peers = 0
    for d in range(1, 2 * chips):
        pl.semaphore_signal(barrier, inc=1, device_id={"tensor": lax.rem(t + d, 2 * chips)}, device_id_type=MESH)
        peers += 1
    for d in range(1, replicas):
        pl.semaphore_signal(barrier, inc=1, device_id={"replica": lax.rem(z + d, replicas)}, device_id_type=MESH)
        peers += 1
    for d in range(1, groups):
        pl.semaphore_signal(barrier, inc=1, device_id={"groups": lax.rem(y + d, groups)}, device_id_type=MESH)
        peers += 1

    order = list(range(1, chips)) + [0]

    loads = {}
    for d in order:
        for j, who in ((0, 1 - core), (1, core)):
            start = pl.multiple_of((chip_at(d) * 2 + who) * cols, cols)
            loads["k", d, j] = pltpu.make_async_copy(
                k_hbm.at[:, pl.ds(start, cols)],
                kbuf.at[d, :, pl.ds(j * cols, cols)],
                k_sem.at[d, j],
            )
    for m in range(chunks):
        loads["x", m] = pltpu.make_async_copy(
            x_hbm.at[pl.ds(m * step, step)], xbuf.at[pl.ds(m * step, step)], x_sem.at[m]
        )
    loads["down"] = pltpu.make_async_copy(down_hbm, downs.at[z], own_sem.at[0])
    loads["up"] = pltpu.make_async_copy(up_hbm, ups.at[z], own_sem.at[1])
    first = order[0]
    loads["k", first, 0].start()
    loads["k", first, 1].start()
    for m in range(chunks):
        loads["x", m].start()
    for d in order[1:]:
        loads["k", d, 0].start()
        loads["k", d, 1].start()
    loads["down"].start()
    loads["up"].start()

    block_of = lax.broadcasted_iota(jnp.int32, (span_rows, TOGETHER * rank), 1) // rank
    for q in range(requests):
        rowadapter[pl.ds(q * span_rows, span_rows), :] = jnp.full((span_rows, TOGETHER * rank), adapter_ref[q], jnp.int32) - block_of
        angles[pl.ds(q, 1), :] = jnp.full((1, HEAD), span_ref[q] * span_rows, jnp.int32).astype(jnp.float32)
    lane = lax.broadcasted_iota(jnp.int32, (1, HEAD), 1)
    half = HEAD // 2
    index = jnp.where(lane >= half, lane - half, lane).astype(jnp.float32)
    freq = jnp.exp(index * (-2.0 / HEAD * math.log(THETA)))
    sign = jnp.where(lane >= half, 1.0, -1.0)
    start_angle = angles[...] * freq
    row_angle = lax.broadcasted_iota(jnp.int32, (span_rows, HEAD), 0).astype(jnp.float32) * freq
    cos_a, sin_a = jnp.cos(start_angle), jnp.sin(start_angle)
    cos_b, sin_b = jnp.cos(row_angle), jnp.sin(row_angle)
    for q in range(requests):
        rs = pl.ds(q * span_rows, span_rows)
        ca, sa = cos_a[q : q + 1, :], sin_a[q : q + 1, :]
        cosine[rs, :] = ca * cos_b - sa * sin_b
        sine[rs, :] = sign * (sa * cos_b + ca * sin_b)

    def product(d, m):
        if (d, m) == (order[0], 0):
            loads["k", d, 0].wait()
            loads["k", d, 1].wait()
        elif m == 0:
            loads["k", d, 0].wait()
            loads["k", d, 1].wait()
        if d == order[0]:
            loads["x", m].wait()
        rs = pl.ds(m * step, step)
        both = jnp.dot(xbuf[rs, :], kbuf[d], preferred_element_type=jnp.float32)
        osend[d, rs, :] = both[:, :cols].astype(jnp.bfloat16)
        mine[d, rs, :] = both[:, cols:]

    todo = [(d, m) for d in order for m in range(chunks)]
    pl.semaphore_wait(barrier, peers)

    def piece(g, p):
        at = lax.rem(y + g + groups, groups) * part + p * (part // pieces)
        return pl.ds(pl.multiple_of(at, 128), part // pieces)

    def group_part(g):
        return pl.ds(pl.multiple_of(lax.rem(y + g + groups, groups) * part, 128), part)

    def hop(a, p, way):
        return pltpu.make_async_remote_copy(
            src_ref=downs.at[a, :, piece(0, p)], dst_ref=downs.at[a, :, piece(0, p)],
            send_sem=down_ssem.at[a, p, (way + 1) // 2], recv_sem=down_rsem.at[a, p],
            device_id={"replica": z + way}, device_id_type=MESH,
        )

    def own_hop(p, way):
        return pltpu.make_async_remote_copy(
            src_ref=down_hbm.at[:, piece(0, p)], dst_ref=downs.at[z, :, piece(0, p)],
            send_sem=down_ssem.at[z, p, (way + 1) // 2], recv_sem=down_rsem.at[z, p],
            device_id={"replica": z + way}, device_id_type=MESH,
        )

    def forward(a, g, p, own):
        cut = piece(0 if own else -g, p)
        return pltpu.make_async_remote_copy(
            src_ref=downs.at[a, :, cut], dst_ref=downs.at[a, :, cut],
            send_sem=fwd_ssem.at[a, g, p], recv_sem=fwd_rsem.at[a, g, p],
            device_id={"groups": lax.rem(y + g, groups)}, device_id_type=MESH,
        )

    def relay(a, p, way):
        hop(a, p, way).wait_recv()
        pl.when((z + way >= 0) & (z + way < replicas))(lambda: hop(a, p, way).start())
        for g in range(1, groups):
            forward(a, g, p, True).start()

    def relay_from(k):
        for p in range(pieces):
            pl.when(z >= k)(lambda: relay(z - k, p, 1))
            pl.when(z + k < replicas)(lambda: relay(z + k, p, -1))

    def relay_end(k):
        for p in range(pieces):
            @pl.when((z >= k) & (z + 1 < replicas))
            def _():
                (own_hop(p, 1) if k == 0 else hop(z - k, p, 1)).wait_send()

            @pl.when((z + k < replicas) & (z >= 1))
            def _():
                (own_hop(p, -1) if k == 0 else hop(z + k, p, -1)).wait_send()

    def up_send(j):
        return pltpu.make_async_remote_copy(
            src_ref=up_hbm, dst_ref=ups.at[z],
            send_sem=up_ssem.at[j], recv_sem=up_rsem.at[j],
            device_id={"replica": lax.rem(z + j, replicas)}, device_id_type=MESH,
        )

    def up_arrival(j):
        return pltpu.make_async_remote_copy(
            src_ref=up_hbm, dst_ref=ups.at[lax.rem(z - j + replicas, replicas)],
            send_sem=up_ssem.at[j], recv_sem=up_rsem.at[j],
            device_id={"replica": lax.rem(z + j, replicas)}, device_id_type=MESH,
        )

    for p in range(pieces):
        pl.when(z + 1 < replicas)(lambda: own_hop(p, 1).start())
        pl.when(z >= 1)(lambda: own_hop(p, -1).start())

    def to_partner(d, m):
        rs = pl.ds(m * step, step)
        return pltpu.make_async_remote_copy(
            src_ref=osend.at[d, rs], dst_ref=orecv.at[d, rs],
            send_sem=o_ssem.at[d, m], recv_sem=o_rsem.at[d, m],
            device_id={"tensor": partner}, device_id_type=MESH,
        )

    def to_chip(d, m):
        rs = pl.ds(m * step, step)
        return pltpu.make_async_remote_copy(
            src_ref=xsend.at[d, rs], dst_ref=xrecv.at[d, rs],
            send_sem=xs_sem.at[d, m], recv_sem=xr_sem.at[d, m],
            device_id={"tensor": chip_at(d) * 2 + core}, device_id_type=MESH,
        )

    def pass_on(d, m):
        rs = pl.ds(m * step, step)
        to_partner(d, m).wait()
        if d != 0:
            total = mine[d, rs, :] + orecv[d, rs, :].astype(jnp.float32)
            xsend[d, rs, :] = total.astype(jnp.bfloat16)
            to_chip(d, m).start()

    hops = 1
    for i, (d, m) in enumerate(todo):
        product(d, m)
        to_partner(d, m).start()
        if i >= 1:
            pass_on(*todo[i - 1])
        if i + 1 >= chunks and hops < replicas:
            relay_from(hops)
            hops += 1
    for k in range(hops, replicas):
        relay_from(k)
    for j in range(1, replicas):
        up_send(j).start()
    pass_on(*todo[-1])

    def shrink(cut):
        kept = None
        for a in range(0, replicas, TOGETHER):
            value = lax.dot_general(
                xbuf[:, cut],
                downs[a : a + TOGETHER, :, cut].reshape(TOGETHER * rank, part),
                (((1,), (1,)), ((), ())),
                preferred_element_type=jnp.float32,
            )
            chosen = jnp.where(rowadapter[...] == a, value, 0.0)
            kept = chosen if kept is None else kept + chosen
        pair = kept[:, : 2 * rank] + kept[:, 2 * rank :]
        return pair + pltpu.roll(pair, rank, 1)

    loads["down"].wait()
    zacc[...] = shrink(group_part(0))
    for m in range(chunks):
        rs = pl.ds(m * step, step)
        base = mine[0, rs, :] + orecv[0, rs, :].astype(jnp.float32)
        for d in range(1, chips):
            to_chip(d, m).wait()
            base += xrecv[d, rs, :].astype(jnp.float32)
        mine[0, rs, :] = base
    for g in range(1, groups):
        for j in range(1, replicas):
            for p in range(pieces):
                forward(lax.rem(z + j, replicas), g, p, False).wait_recv()
    for g in range(1, groups):
        zacc[...] += shrink(group_part(-g))

    mid = rows // 2
    quarter = rows // 4
    low = lax.broadcasted_iota(jnp.int32, (mid, 2 * rank), 1) < rank
    packed = jnp.where(low, zacc[:mid, :], zacc[mid:, :])
    for h in range(2):
        zsend[h] = packed[h * quarter : (h + 1) * quarter].astype(jnp.bfloat16)
    def z_copy(i):
        given, taken = ((1 - core, core), (core, 1 - core))[i]
        return [
            pltpu.make_async_remote_copy(
                src_ref=zsend.at[h], dst_ref=zrecv.at[h], send_sem=z_ssem.at[i], recv_sem=z_rsem.at[i],
                device_id={"tensor": partner}, device_id_type=MESH,
            )
            for h in (given, taken)
        ]

    for i in range(2):
        z_copy(i)[0].start()
    z_copy(0)[1].wait_recv()
    zchip[core] = (zsend[core].astype(jnp.float32) + zrecv[core].astype(jnp.float32)).astype(jnp.bfloat16)

    def z_over(d, c):
        return pltpu.make_async_remote_copy(
            src_ref=zchip.at[core], dst_ref=zx.at[d, core],
            send_sem=zx_ssem.at[d, c], recv_sem=zx_rsem.at[d, core],
            device_id={"tensor": chip_at(d) * 2 + c}, device_id_type=MESH,
        )

    def z_arrival(d, c):
        return pltpu.make_async_remote_copy(
            src_ref=zchip.at[c], dst_ref=zx.at[d, c],
            send_sem=zx_ssem.at[d, c], recv_sem=zx_rsem.at[d, c],
            device_id={"tensor": chip_at(d) * 2 + c}, device_id_type=MESH,
        )

    for d in range(1, chips):
        for c in range(2):
            z_over(d, c).start()
    z_copy(1)[1].wait_recv()
    for i in range(2):
        z_copy(i)[0].wait_send()
    chip_sum = [
        packed[h * quarter : (h + 1) * quarter] + zrecv[h].astype(jnp.float32) for h in range(2)
    ]
    loads["up"].wait()
    for j in range(1, replicas):
        up_arrival(j).wait()
    for k in range(replicas):
        relay_end(k)
    for g in range(1, groups):
        for j in range(1, replicas):
            for p in range(pieces):
                forward(lax.rem(z + j, replicas), g, p, True).wait_send()
    for d in range(1, chips):
        for c in range(2):
            z_arrival(d, c).wait()
    sums = []
    for h in range(2):
        total = chip_sum[h]
        for d in range(1, chips):
            total = total + zx[d, h].astype(jnp.float32)
        sums.append(total)
    packed = jnp.concatenate(sums, axis=0)
    swapped = pltpu.roll(packed, rank, 1)
    shrunk = jnp.concatenate([jnp.where(low, packed, swapped), jnp.where(low, swapped, packed)], axis=0)
    shrunk = jnp.concatenate([shrunk] * (TOGETHER // 2), axis=1)

    for m in range(chunks):
        rs = pl.ds(m * step, step)
        reduced = shrunk[m * step : (m + 1) * step]
        names = rowadapter[rs, :]
        expanded = jnp.zeros((step, cols), jnp.float32)
        for a in range(0, replicas, TOGETHER):
            expanded += jnp.dot(
                jnp.where(names == a, reduced, 0.0).astype(jnp.bfloat16),
                ups[a : a + TOGETHER].reshape(TOGETHER * rank, cols),
                preferred_element_type=jnp.float32,
            )
        delta = (expanded * SCALE).astype(jnp.bfloat16).astype(jnp.float32)
        before = mine[0, rs, :] + delta
        for h in range(cols // HEAD):
            head = before[:, h * HEAD : (h + 1) * HEAD]
            turned = head * cosine[rs, :] + pltpu.roll(head, half, 1) * sine[rs, :]
            out_ref[rs, h * HEAD : (h + 1) * HEAD] = turned.astype(jnp.bfloat16)


def on_device(sizes, rows, adapters, spans, keys, down, up):
    groups, replicas, chips, chunks, pieces = sizes
    row_count, width = rows.shape
    rank, cols = up.shape[1], up.shape[2]
    requests = spans.shape[0]
    bf, f32 = jnp.bfloat16, jnp.float32
    vm, dma = pltpu.VMEM, pltpu.SemaphoreType.DMA
    quarter = row_count // 4
    anywhere = pl.BlockSpec(memory_space=pltpu.HBM)
    smem = pl.BlockSpec(memory_space=pltpu.SMEM)
    return pl.pallas_call(
        functools.partial(kernel, sizes),
        out_shape=jax.ShapeDtypeStruct((row_count, cols), bf),
        in_specs=[anywhere, smem, smem, anywhere, anywhere, anywhere],
        out_specs=pl.BlockSpec(memory_space=pltpu.VMEM),
        scratch_shapes=[
            vm((row_count, width), bf),
            vm((chips, width, 2 * cols), bf),
            vm((replicas, rank, width), bf),
            vm((replicas, rank, cols), bf),
            vm((chips, row_count, cols), f32),
            vm((chips, row_count, cols), bf),
            vm((chips, row_count, cols), bf),
            vm((chips, row_count, cols), bf),
            vm((chips, row_count, cols), bf),
            vm((row_count, 2 * rank), f32),
            vm((2, quarter, 2 * rank), bf),
            vm((2, quarter, 2 * rank), bf),
            vm((2, quarter, 2 * rank), bf),
            vm((chips, 2, quarter, 2 * rank), bf),
            vm((row_count, TOGETHER * rank), jnp.int32),
            vm((row_count, HEAD), f32),
            vm((row_count, HEAD), f32),
            vm((requests, HEAD), f32),
            dma((chunks,)), dma((chips, 2)), dma((2,)),
            dma((replicas, pieces, 2)), dma((replicas, pieces)),
            dma((replicas, groups, pieces)), dma((replicas, groups, pieces)),
            dma((replicas,)), dma((replicas,)),
            dma((chips, chunks)), dma((chips, chunks)),
            dma((chips, chunks)), dma((chips, chunks)),
            dma((2,)), dma((2,)),
            dma((chips, 2)), dma((chips, 2)),
        ],
        compiler_params=pltpu.CompilerParams(
            collective_id=0, has_side_effects=True, vmem_limit_bytes=60 * 1024 * 1024
        ),
        cost_estimate=pl.CostEstimate(
            flops=2 * row_count * width * (2 * chips * cols + replicas * rank),
            bytes_accessed=2 * width * (row_count + 2 * chips * cols),
            transcendentals=0,
        ),
    )(rows, adapters.reshape(requests), spans, keys, down[0].T, up[0])


def solution(mesh):
    in_specs = (
        P(("groups", "replica"), "tensor"),
        P(("groups", "replica"), None),
        P(("groups", "replica")),
        P("tensor", None),
        P("replica", "tensor", None),
        P("replica", None, "tensor"),
    )
    out_specs = P(("groups", "replica"), "tensor")
    sizes = (mesh.shape["groups"], mesh.shape["replica"], mesh.shape["tensor"] // 2, 3)
    sizes += (max(1, 16 // sizes[1]),)
    return jax.shard_map(
        functools.partial(on_device, sizes), mesh=mesh, in_specs=in_specs, out_specs=out_specs, check_vma=False
    )
```
